32 devices in a mesh: mem: 4 (over y, core), gx: 8 (over z, x).
Axes of the slice: x: 2, y: 2, z: 4, core: 2. Of those that a mesh axis runs over, the one named last changes fastest.
Arguments:
- weights: bfloat16 [4, 128, 32768], P('mem', 'gx'), may hold values from -6 to 6
- perturbations: bfloat16 [2, 4, 128, 32768], P(None, 'mem', 'gx'), may hold values from -3 to 3
- obs_cell: int32 [32768], P('gx'), may hold values from 0 to 524287
- obs_slot: int32 [32768], P('gx'), may hold values from 0 to 1
- innovation: float32 [32768], P('gx'), may hold values from -24 to 24
- obs_weight: float32 [32768], P('gx'), may hold values from 0.5 to 4
- obs_count: int32 [8], P('gx'), may hold values from 2048 to 4096, as said below
Outputs:
- gradient: float32 [4, 128, 32768], P('mem', 'gx')
The draws below stay inside these ranges and needn't reach their ends.
Inputs may be any that keep to these rules, and one draw needn't show every extreme that they name: Slab s uses its first obs_count[s] observation slots, o = s * 4096 .. s * 4096 + obs_count[s] - 1; some slab is full and another holds 2048. `obs_cell`: the cell is numbered (x within the slab) * 512 * 64 + y * 64 + z; several observations may share a cell.
All inputs are finite; a program needn't handle non-finite values.
Results may differ from the reference program's by a relative error of at most 0.0029.
Values may be sent and summed in bfloat16 or wider, within the bound.
A program may use at most 64 MiB of HBM per device.

```python
import math
import jax
import jax.numpy as jnp
from jax import lax

CX = 16
NY = 512
NZ = 64
TS = 2
OBS_DEV = 4096
MEMBERS = 4
NX = 128
SLABS = 8
NOBS = 32768


def draw_obs_count(key, part):
    first_key, second_key = jax.random.split(jax.random.fold_in(key, 17))
    base_counts = jax.random.randint(first_key, (SLABS,), OBS_DEV // 2, OBS_DEV + 1)
    full_slab = jax.random.randint(second_key, (), 0, SLABS)
    half_slab = (full_slab + 1) % SLABS
    positions = jnp.arange(SLABS)
    counts = jnp.where(positions == full_slab, OBS_DEV, base_counts)
    counts = jnp.where(positions == half_slab, OBS_DEV // 2, counts)
    return counts.astype(jnp.int32)


def set_ends(result, key, smallest, high):
    spot = [jax.random.randint(jax.random.fold_in(key, axis), (), 0, length) for axis, length in enumerate(result.shape)]
    longest = result.shape.index(max(result.shape))
    beside = spot[:longest] + [(spot[longest] + 1) % result.shape[longest]] + spot[longest + 1:]
    return result.at[tuple(spot)].set(smallest).at[tuple(beside)].set(high)


def block_scale(rng, extent, pieces, low, top_value):
    def one(axis_at, parts):
        steps = jax.random.uniform(jax.random.fold_in(jax.random.fold_in(rng, 6), axis_at), (parts,), jnp.float32, low / len(pieces), top_value / len(pieces))
        return jnp.repeat(jnp.exp(steps), extent[axis_at] // parts).reshape((-1,) + (1,) * (len(extent) - axis_at - 1))

    loudness = one(*pieces[0])
    for cut in pieces[1:]:
        loudness = loudness * one(*cut)
    return loudness


def centred(key, shape, scale, limit, cuts=(), dtype=jnp.bfloat16):
    gain = block_scale(key, shape, cuts, -0.22, 0.18) if cuts else 1.0
    entries = jax.random.normal(key, shape, jnp.float32) * scale * gain
    return jnp.minimum(jnp.maximum(entries, -limit), limit).astype(dtype)


def setup_inputs(seed: int = 0) -> dict:
    seeds = jax.random.split(jax.random.key(seed), 8)
    weights = centred(seeds[0], (MEMBERS, NX, NY * NZ), 1.0, 6.0, ((0, 4), (1, 8)))
    perturbations = centred(seeds[1], (TS, MEMBERS, NX, NY * NZ), 0.5, 3.0, ((1, 4), (2, 8)))
    obs_cell = set_ends(jax.random.randint(seeds[2], (NOBS,), 0, CX * NY * NZ), jax.random.fold_in(seeds[2], 1), 0, (CX * NY * NZ) - 1).astype(jnp.int32)
    obs_slot = set_ends(jax.random.randint(seeds[3], (NOBS,), 0, TS), jax.random.fold_in(seeds[3], 1), 0, TS - 1).astype(jnp.int32)
    innovation = centred(seeds[4], (NOBS,), 4.0, 24.0, ((0, 8),), jnp.float32)
    obs_weight = jnp.clip(jnp.exp(math.log(4.0) - 2.0794415 * jax.random.uniform(seeds[5], (NOBS,), jnp.float32) ** block_scale(seeds[5], (NOBS,), ((0, 8),), -0.2, 0.2)), 0.5, 4.0)
    obs_count = draw_obs_count(jax.random.fold_in(seeds[7], 71), 0)
    return {"weights": weights, "perturbations": perturbations, "obs_cell": obs_cell, "obs_slot": obs_slot, "innovation": innovation, "obs_weight": obs_weight, "obs_count": obs_count}


tap_reach = 15
corr_scale = 7.0

def tap_values():
    offsets = jnp.arange(-tap_reach, tap_reach + 1).astype(jnp.float32)
    bell = jnp.exp(-offsets * offsets / (2.0 * corr_scale * corr_scale))
    return (bell / jnp.sqrt(jnp.sum(bell * bell))).astype(jnp.bfloat16)

def square_band(count):
    positions = jnp.arange(count)
    offsets = positions[None, :] - positions[:, None]
    tap_table = tap_values()
    lookup = tap_table[jnp.clip(offsets + tap_reach, 0, 2 * tap_reach)]
    return jnp.where(jnp.abs(offsets) <= tap_reach, lookup, jnp.zeros_like(lookup))

def reference(weights, perturbations, obs_cell, obs_slot, innovation, obs_weight, obs_count):
    plane_cells = NY * NZ
    band_z = square_band(NZ).astype(jnp.float32)
    band_y = square_band(NY).astype(jnp.float32)
    tap_table = tap_values()

    def along_z(field):
        grid = field.reshape(NX, NY, NZ).astype(jnp.float32)
        return jnp.einsum('xyq,zq->xyz', grid, band_z).reshape(NX, plane_cells)

    def along_y(field):
        grid = field.reshape(NX, NY, NZ).astype(jnp.float32)
        return jnp.einsum('xqz,yq->xyz', grid, band_y).reshape(NX, plane_cells)

    def along_x(field):
        padded = jnp.pad(field.astype(jnp.float32), ((tap_reach, tap_reach), (0, 0)))
        running = jnp.zeros((NX, plane_cells), jnp.float32)
        for shift_index in range(2 * tap_reach + 1):
            running = running + tap_table[shift_index].astype(jnp.float32) * padded[shift_index:shift_index + NX]
        return running
    pert_members = jnp.moveaxis(perturbations, 1, 0)

    def forward(carry, item):
        weight_k, pert_k = item
        z_smooth = along_z(weight_k).astype(jnp.bfloat16)
        y_smooth = along_y(z_smooth).astype(jnp.bfloat16)
        smoothed = along_x(y_smooth)
        return (carry + pert_k.astype(jnp.float32) * smoothed[None], None)
    increment, _ = lax.scan(forward, jnp.zeros((TS, NX, plane_cells), jnp.float32), (weights, pert_members))
    obs_order = jnp.arange(NOBS).astype(jnp.int32)
    slab = obs_order // OBS_DEV
    rows = (slab * CX + obs_cell // plane_cells).astype(jnp.int32)
    columns = (obs_cell % plane_cells).astype(jnp.int32)
    live_mask = (obs_order % OBS_DEV < obs_count[slab]).astype(jnp.float32)
    sampled = increment[obs_slot, rows, columns]
    residual = live_mask * obs_weight * (sampled - innovation)
    forcing = jnp.zeros((TS, NX, plane_cells), jnp.float32).at[obs_slot, rows, columns].add(residual)

    def backward(item):
        weight_k, pert_k = item
        adjoint_source = lax.optimization_barrier(jnp.sum(pert_k.astype(jnp.float32) * forcing, axis=0)).astype(jnp.bfloat16)
        x_back = along_x(adjoint_source).astype(jnp.bfloat16)
        y_back = along_y(x_back).astype(jnp.bfloat16)
        return weight_k.astype(jnp.float32) + along_z(y_back)
    return lax.map(backward, (weights, pert_members))
```

```python
import functools

import ml_dtypes
import numpy as np

import jax
import jax.numpy as jnp
from jax import lax
from jax.experimental import pallas as pl
from jax.experimental.pallas import tpu as pltpu
from jax.sharding import PartitionSpec as P

NY = 512
NZ = 64
REACH = 15
LANES = 128
PAIRS = NY // 2
LOW = 64
HIGH = PAIRS // LOW
VMEM_LIMIT = 56 * 1024 * 1024
NT = (((1,), (1,)), ((), ()))


def tap_values():
    j = np.arange(-REACH, REACH + 1).astype(np.float32)
    bell = np.exp(-j * j / np.float32(98.0))
    return (bell / np.sqrt(np.sum(bell * bell))).astype(ml_dtypes.bfloat16)


def taps_at(offset):
    taps = tap_values()
    look = taps[np.clip(offset + REACH, 0, 2 * REACH)]
    return np.where(np.abs(offset) <= REACH, look, np.zeros_like(look))


def z_band():
    z = np.arange(LANES) % NZ
    half = np.arange(LANES) // NZ
    band = taps_at(z[:, None] - z[None, :])
    return np.where(half[:, None] == half[None, :], band, np.zeros_like(band))


def y_band(rows):
    out_c, out_x = np.arange(16 * rows) // rows, np.arange(16 * rows) % rows
    in_c, in_x = np.arange(32 * rows) // rows - 8, np.arange(32 * rows) % rows
    step = 2 * (in_c[None, :] - out_c[:, None])
    same = out_x[:, None] == in_x[None, :]
    parts = []
    for shift in (0, 1, -1):
        band = taps_at(step + shift)
        parts.append(np.where(same, band, np.zeros_like(band)))
    return np.concatenate(parts, axis=1)


def x_bands(rows):
    x = np.arange(rows)
    return np.stack([taps_at(x[:, None] - (x[None, :] + off)) for off in (0, -rows, rows)])


def split_cell(cell):
    x = cell >> 15
    pair = (cell >> 7) & (PAIRS - 1)
    low = pair & (LOW - 1)
    row = (pair // LOW) * LANES + (cell & (LANES - 1))
    return x, low, row


def fill_a(a_ref, x_rows, low, rows):
    count = x_rows.shape[1]
    low_b = jnp.broadcast_to(low.astype(jnp.float32), (rows, count)).astype(jnp.bfloat16)
    zero = jnp.zeros_like(x_rows)
    for c in range(LOW):
        a_ref[c * rows:(c + 1) * rows, :] = jnp.where(low_b == jnp.bfloat16(c), x_rows, zero)


def x_taps(kx, x, rows):
    hot = (lax.broadcasted_iota(jnp.int32, (rows, x.shape[1]), 0) == x)
    hot = hot.astype(jnp.float32).astype(jnp.bfloat16)
    if kx is None:
        return hot
    return jnp.dot(kx, hot, preferred_element_type=jnp.float32).astype(jnp.bfloat16)


def pairs_block(w_ref, b, rows):
    parts = []
    for j in range(16):
        start = pl.multiple_of((b * 16 + j) * LANES, LANES)
        parts.append(w_ref[:, pl.ds(start, LANES)])
    return jnp.concatenate(parts, axis=0)


def sample_kernel(block, w_ref, cell_ref, kz_ref, kyt_ref, kx_ref, s_ref, z_ref, y_ref, a_ref):
    rows = w_ref.shape[0]
    span = 16 * rows
    pad = 8 * rows
    depth = LOW * rows
    z_ref[:, :pad] = jnp.zeros((LANES, pad), jnp.bfloat16)
    z_ref[:, pad + PAIRS * rows:] = jnp.zeros((LANES, pad), jnp.bfloat16)

    @pl.loop(0, PAIRS // 16)
    def _(b):
        part = pairs_block(w_ref, b, rows)
        z = lax.dot_general(kz_ref[...], part, NT, preferred_element_type=jnp.float32)
        z_ref[:, pl.ds(pl.multiple_of(pad + b * span, LANES), span)] = z.astype(jnp.bfloat16)

    @pl.loop(0, PAIRS // 16)
    def _(b):
        win = z_ref[:, pl.ds(pl.multiple_of(b * span, LANES), 2 * span)]
        top, bottom = win[:NZ], win[NZ:]
        none = jnp.zeros_like(top)
        from_bottom = jnp.concatenate([bottom, none], axis=0)
        from_top = jnp.concatenate([none, top], axis=0)
        wide = jnp.concatenate([win, from_bottom, from_top], axis=1)
        y = jnp.dot(wide, kyt_ref[...], preferred_element_type=jnp.float32)
        high = b // (LOW // 16)
        col = pl.multiple_of((b % (LOW // 16)) * span, LANES)
        y_ref[pl.ds(pl.multiple_of(high * LANES, LANES), LANES), pl.ds(col, span)] = y.astype(
            jnp.bfloat16)

    per_list = cell_ref.shape[1] // 3

    @pl.loop(0, cell_ref.shape[1] // block)
    def _(i):
        at = pl.ds(pl.multiple_of(i * block, block), block)
        x, low, row = split_cell(cell_ref[:, at])
        kx = kx_ref[i // (per_list // block)]
        fill_a(a_ref, x_taps(kx, x, rows), low, rows)
        m = jnp.dot(y_ref[...], a_ref[...], preferred_element_type=jnp.float32)
        hit = lax.broadcasted_iota(jnp.int32, m.shape, 0) == row
        s_ref[:, at] = jnp.sum(jnp.where(hit, m, 0.0), axis=0, keepdims=True)


def pick_kernel(block, p_ref, cell_ref, slot_ref, eye_ref, o_ref, t_ref, a_ref):
    slots, rows = p_ref.shape[:2]
    span = 16 * rows

    for t in range(slots):
        @pl.loop(0, PAIRS // 16)
        def _(b):
            part = pairs_block(p_ref.at[t], b, rows)
            z = lax.dot_general(eye_ref[...], part, NT, preferred_element_type=jnp.float32)
            high = b // (LOW // 16)
            col = pl.multiple_of((b % (LOW // 16)) * span, LANES)
            row0 = pl.multiple_of((t * HIGH + high) * LANES, LANES)
            t_ref[pl.ds(row0, LANES), pl.ds(col, span)] = z.astype(jnp.bfloat16)

    @pl.loop(0, cell_ref.shape[1] // block)
    def _(i):
        at = pl.ds(pl.multiple_of(i * block, block), block)
        x, low, row = split_cell(cell_ref[:, at])
        row = row + slot_ref[:, at] * (HIGH * LANES)
        fill_a(a_ref, x_taps(None, x, rows), low, rows)
        m = jnp.dot(t_ref[...], a_ref[...], preferred_element_type=jnp.float32)
        hit = lax.broadcasted_iota(jnp.int32, m.shape, 0) == row
        o_ref[:, at] = jnp.sum(jnp.where(hit, m, 0.0), axis=0, keepdims=True)


def back_kernel(block, w_ref, cell_ref, v_ref, kz_ref, ky_ref, kx_ref, out_ref,
                g_ref, x_ref, a_ref, b_ref):
    rows = w_ref.shape[0]
    span = 16 * rows
    pad = 8 * rows
    depth = LOW * rows
    per_list = cell_ref.shape[1] // 3
    g_ref[...] = jnp.zeros_like(g_ref)

    @pl.loop(0, cell_ref.shape[1] // block)
    def _(i):
        at = pl.ds(pl.multiple_of(i * block, block), block)
        x, low, row = split_cell(cell_ref[:, at])
        kx = kx_ref[i // (per_list // block)]
        fill_a(a_ref, x_taps(kx, x, rows), low, rows)
        shape = (HIGH * LANES, block)
        hit = lax.broadcasted_iota(jnp.int32, shape, 0) == row
        b_ref[...] = jnp.where(hit, v_ref[:, at], 0.0).astype(jnp.bfloat16)
        g_ref[...] += lax.dot_general(
            a_ref[...], b_ref[...], NT, preferred_element_type=jnp.float32)

    x_ref[:pad, :] = jnp.zeros((pad, LANES), jnp.bfloat16)
    x_ref[pad + PAIRS * rows:, :] = jnp.zeros((pad, LANES), jnp.bfloat16)
    for h in range(HIGH):
        x_ref[pad + h * depth:pad + (h + 1) * depth, :] = g_ref[
            :, h * LANES:(h + 1) * LANES].astype(jnp.bfloat16)

    @pl.loop(0, PAIRS // 16)
    def _(b):
        win = x_ref[pl.ds(pl.multiple_of(b * span, LANES), 2 * span), :]
        first, second = win[:, :NZ], win[:, NZ:]
        none = jnp.zeros_like(first)
        from_second = jnp.concatenate([second, none], axis=1)
        from_first = jnp.concatenate([none, first], axis=1)
        tall = jnp.concatenate([win, from_second, from_first], axis=0)
        y = jnp.dot(ky_ref[...], tall, preferred_element_type=jnp.float32)
        z = jnp.dot(y.astype(jnp.bfloat16), kz_ref[...], preferred_element_type=jnp.float32)
        for j in range(16):
            lane = pl.ds(pl.multiple_of((b * 16 + j) * LANES, LANES), LANES)
            out_ref[:, lane] = z[j * rows:(j + 1) * rows] + w_ref[:, lane].astype(jnp.float32)


def vmem(count):
    return [pl.BlockSpec(memory_space=pltpu.VMEM)] * count


def local(weights, perturbations, obs_cell, obs_slot, innovation, obs_weight, obs_count):
    rows, plane = weights.shape[1:]
    slots = perturbations.shape[0]
    count = obs_cell.shape[0]
    w = weights[0]
    pert = perturbations[:, 0]
    depth = LOW * rows
    wide = HIGH * LANES
    padded = (PAIRS + 16) * rows
    params = pltpu.CompilerParams(vmem_limit_bytes=VMEM_LIMIT)
    bf16 = jnp.bfloat16

    slabs = lax.axis_size("gx")
    forward = [(i, i + 1) for i in range(slabs - 1)]
    backward = [(b, a) for a, b in forward]

    kz = jnp.asarray(z_band())
    ky_np = y_band(rows)
    ky, kyt = jnp.asarray(ky_np), jnp.asarray(np.ascontiguousarray(ky_np.T))
    kx = jnp.asarray(x_bands(rows))
    eye = jnp.asarray(np.eye(LANES).astype(ml_dtypes.bfloat16))

    cell_left = lax.ppermute(obs_cell, "gx", forward)
    cell_right = lax.ppermute(obs_cell, "gx", backward)
    cell = obs_cell.reshape(1, count)
    slot = obs_slot.reshape(1, count)
    cells = jnp.concatenate([obs_cell, cell_left, cell_right]).reshape(1, 3 * count)

    block = 512
    picked = pl.pallas_call(
        functools.partial(pick_kernel, block),
        out_shape=jax.ShapeDtypeStruct((1, count), jnp.float32),
        in_specs=vmem(4),
        out_specs=vmem(1)[0],
        scratch_shapes=[
            pltpu.VMEM((slots * wide, depth), bf16),
            pltpu.VMEM((depth, block), bf16),
        ],
        compiler_params=params,
        cost_estimate=pl.CostEstimate(
            flops=2 * slots * rows * plane * count, bytes_accessed=4 * rows * plane,
            transcendentals=0),
        name="pick",
    )(pert, cell, slot, eye)

    sampled3 = pl.pallas_call(
        functools.partial(sample_kernel, block),
        out_shape=jax.ShapeDtypeStruct((1, 3 * count), jnp.float32),
        in_specs=vmem(5),
        out_specs=vmem(1)[0],
        scratch_shapes=[
            pltpu.VMEM((LANES, padded), bf16),
            pltpu.VMEM((wide, depth), bf16),
            pltpu.VMEM((depth, block), bf16),
        ],
        compiler_params=params,
        cost_estimate=pl.CostEstimate(
            flops=6 * rows * plane * count, bytes_accessed=2 * rows * plane, transcendentals=0),
        name="sample",
    )(w, cells, kz, kyt, kx)[0]
    own, for_left, for_right = sampled3[:count], sampled3[count:2 * count], sampled3[2 * count:]
    own = own + lax.ppermute(for_left, "gx", backward) + lax.ppermute(for_right, "gx", forward)

    picked = picked[0]
    share = picked * own
    members = lax.axis_size("mem")
    sampled = share
    for step in range(1, members):
        sampled = sampled + lax.ppermute(
            share, "mem", [(i, (i + step) % members) for i in range(members)])
    live_mask = (jnp.arange(count) < obs_count[0]).astype(jnp.float32)
    residual = live_mask * obs_weight * (sampled - innovation)
    source = picked * residual
    source_left = lax.ppermute(source, "gx", forward)
    source_right = lax.ppermute(source, "gx", backward)
    sources = jnp.concatenate([source, source_left, source_right]).reshape(1, 3 * count)

    back_block = 1024
    out = pl.pallas_call(
        functools.partial(back_kernel, back_block),
        out_shape=jax.ShapeDtypeStruct((rows, plane), jnp.float32),
        in_specs=vmem(6),
        out_specs=vmem(1)[0],
        scratch_shapes=[
            pltpu.VMEM((depth, wide), jnp.float32),
            pltpu.VMEM((padded, LANES), bf16),
            pltpu.VMEM((depth, back_block), bf16),
            pltpu.VMEM((wide, back_block), bf16),
        ],
        compiler_params=params,
        cost_estimate=pl.CostEstimate(
            flops=6 * rows * plane * count, bytes_accessed=6 * rows * plane, transcendentals=0),
        name="back",
    )(w, cells, sources, kz, ky, kx)
    return out[None]


def solution(mesh):
    return jax.shard_map(
        local,
        mesh=mesh,
        in_specs=(
            P("mem", "gx", None),
            P(None, "mem", "gx", None),
            P("gx"),
            P("gx"),
            P("gx"),
            P("gx"),
            P("gx"),
        ),
        out_specs=P("mem", "gx", None),
        check_vma=False,
    )
```

```python
import functools

import ml_dtypes
import numpy as np

import jax
import jax.numpy as jnp
from jax import lax
from jax.experimental import pallas as pl
from jax.experimental.pallas import tpu as pltpu
from jax.sharding import PartitionSpec as P

NY = 512
NZ = 64
REACH = 15
LANES = 128
PAIRS = NY // 2
LOW = 64
HIGH = PAIRS // LOW
VMEM_LIMIT = 56 * 1024 * 1024
NT = (((1,), (1,)), ((), ()))
MESH = pl.DeviceIdType.MESH


def tap_values():
    j = np.arange(-REACH, REACH + 1).astype(np.float32)
    bell = np.exp(-j * j / np.float32(98.0))
    return (bell / np.sqrt(np.sum(bell * bell))).astype(ml_dtypes.bfloat16)


def taps_at(offset):
    taps = tap_values()
    look = taps[np.clip(offset + REACH, 0, 2 * REACH)]
    return np.where(np.abs(offset) <= REACH, look, np.zeros_like(look))


def z_band():
    z = np.arange(LANES) % NZ
    half = np.arange(LANES) // NZ
    band = taps_at(z[:, None] - z[None, :])
    return np.where(half[:, None] == half[None, :], band, np.zeros_like(band))


def y_band(rows):
    out_c, out_x = np.arange(16 * rows) // rows, np.arange(16 * rows) % rows
    in_c, in_x = np.arange(32 * rows) // rows - 8, np.arange(32 * rows) % rows
    step = 2 * (in_c[None, :] - out_c[:, None])
    same = out_x[:, None] == in_x[None, :]
    parts = []
    for shift in (0, 1, -1):
        band = taps_at(step + shift)
        parts.append(np.where(same, band, np.zeros_like(band)))
    return np.concatenate(parts, axis=1)


def x_bands(rows):
    x = np.arange(rows)
    return np.stack([taps_at(x[:, None] - (x[None, :] + off)) for off in (0, -rows, rows)])


def split_cell(cell):
    x = cell >> 15
    pair = (cell >> 7) & (PAIRS - 1)
    low = pair & (LOW - 1)
    row = (pair // LOW) * LANES + (cell & (LANES - 1))
    return x, low, row


def fill_a(a_ref, x_rows, low, rows):
    count = x_rows.shape[1]
    low_b = jnp.broadcast_to(low.astype(jnp.float32), (rows, count)).astype(jnp.bfloat16)
    zero = jnp.zeros_like(x_rows)
    for c in range(LOW):
        a_ref[c * rows:(c + 1) * rows, :] = jnp.where(low_b == jnp.bfloat16(c), x_rows, zero)


def x_taps(kx, x, rows):
    hot = (lax.broadcasted_iota(jnp.int32, (rows, x.shape[1]), 0) == x)
    hot = hot.astype(jnp.float32).astype(jnp.bfloat16)
    if kx is None:
        return hot
    return jnp.dot(kx, hot, preferred_element_type=jnp.float32).astype(jnp.bfloat16)


def pairs_block(w_ref, b, rows):
    parts = []
    for j in range(16):
        start = pl.multiple_of((b * 16 + j) * LANES, LANES)
        parts.append(w_ref[:, pl.ds(start, LANES)])
    return jnp.concatenate(parts, axis=0)


def sample_kernel(block, w_ref, cell_ref, kz_ref, kyt_ref, kx_ref, s_ref, z_ref, y_ref, a_ref):
    rows = w_ref.shape[0]
    span = 16 * rows
    pad = 8 * rows
    depth = LOW * rows
    z_ref[:, :pad] = jnp.zeros((LANES, pad), jnp.bfloat16)
    z_ref[:, pad + PAIRS * rows:] = jnp.zeros((LANES, pad), jnp.bfloat16)

    @pl.loop(0, PAIRS // 16)
    def _(b):
        part = pairs_block(w_ref, b, rows)
        z = lax.dot_general(kz_ref[...], part, NT, preferred_element_type=jnp.float32)
        z_ref[:, pl.ds(pl.multiple_of(pad + b * span, LANES), span)] = z.astype(jnp.bfloat16)

    @pl.loop(0, PAIRS // 16)
    def _(b):
        win = z_ref[:, pl.ds(pl.multiple_of(b * span, LANES), 2 * span)]
        top, bottom = win[:NZ], win[NZ:]
        none = jnp.zeros_like(top)
        from_bottom = jnp.concatenate([bottom, none], axis=0)
        from_top = jnp.concatenate([none, top], axis=0)
        wide = jnp.concatenate([win, from_bottom, from_top], axis=1)
        y = jnp.dot(wide, kyt_ref[...], preferred_element_type=jnp.float32)
        high = b // (LOW // 16)
        col = pl.multiple_of((b % (LOW // 16)) * span, LANES)
        y_ref[pl.ds(pl.multiple_of(high * LANES, LANES), LANES), pl.ds(col, span)] = y.astype(
            jnp.bfloat16)

    per_list = cell_ref.shape[1] // 3

    @pl.loop(0, cell_ref.shape[1] // block)
    def _(i):
        at = pl.ds(pl.multiple_of(i * block, block), block)
        x, low, row = split_cell(cell_ref[:, at])
        kx = kx_ref[i // (per_list // block)]
        fill_a(a_ref, x_taps(kx, x, rows), low, rows)
        m = jnp.dot(y_ref[...], a_ref[...], preferred_element_type=jnp.float32)
        hit = lax.broadcasted_iota(jnp.int32, m.shape, 0) == row
        s_ref[:, at] = jnp.sum(jnp.where(hit, m, 0.0), axis=0, keepdims=True)


def pick_kernel(block, p_ref, cell_ref, slot_ref, eye_ref, o_ref, t_ref, a_ref):
    slots, rows = p_ref.shape[:2]
    span = 16 * rows

    for t in range(slots):
        @pl.loop(0, PAIRS // 16)
        def _(b):
            part = pairs_block(p_ref.at[t], b, rows)
            z = lax.dot_general(eye_ref[...], part, NT, preferred_element_type=jnp.float32)
            high = b // (LOW // 16)
            col = pl.multiple_of((b % (LOW // 16)) * span, LANES)
            row0 = pl.multiple_of((t * HIGH + high) * LANES, LANES)
            t_ref[pl.ds(row0, LANES), pl.ds(col, span)] = z.astype(jnp.bfloat16)

    @pl.loop(0, cell_ref.shape[1] // block)
    def _(i):
        at = pl.ds(pl.multiple_of(i * block, block), block)
        x, low, row = split_cell(cell_ref[:, at])
        row = row + slot_ref[:, at] * (HIGH * LANES)
        fill_a(a_ref, x_taps(None, x, rows), low, rows)
        m = jnp.dot(t_ref[...], a_ref[...], preferred_element_type=jnp.float32)
        hit = lax.broadcasted_iota(jnp.int32, m.shape, 0) == row
        o_ref[:, at] = jnp.sum(jnp.where(hit, m, 0.0), axis=0, keepdims=True)


def back_kernel(block, w_ref, cell_ref, v_ref, kz_ref, ky_ref, kx_ref, out_ref,
                g_ref, x_ref, a_ref, b_ref):
    rows = w_ref.shape[0]
    span = 16 * rows
    pad = 8 * rows
    depth = LOW * rows
    per_list = cell_ref.shape[1] // 3
    g_ref[...] = jnp.zeros_like(g_ref)

    @pl.loop(0, cell_ref.shape[1] // block)
    def _(i):
        at = pl.ds(pl.multiple_of(i * block, block), block)
        x, low, row = split_cell(cell_ref[:, at])
        kx = kx_ref[i // (per_list // block)]
        fill_a(a_ref, x_taps(kx, x, rows), low, rows)
        shape = (HIGH * LANES, block)
        hit = lax.broadcasted_iota(jnp.int32, shape, 0) == row
        b_ref[...] = jnp.where(hit, v_ref[:, at], 0.0).astype(jnp.bfloat16)
        g_ref[...] += lax.dot_general(
            a_ref[...], b_ref[...], NT, preferred_element_type=jnp.float32)

    x_ref[:pad, :] = jnp.zeros((pad, LANES), jnp.bfloat16)
    x_ref[pad + PAIRS * rows:, :] = jnp.zeros((pad, LANES), jnp.bfloat16)
    for h in range(HIGH):
        x_ref[pad + h * depth:pad + (h + 1) * depth, :] = g_ref[
            :, h * LANES:(h + 1) * LANES].astype(jnp.bfloat16)

    @pl.loop(0, PAIRS // 16)
    def _(b):
        win = x_ref[pl.ds(pl.multiple_of(b * span, LANES), 2 * span), :]
        first, second = win[:, :NZ], win[:, NZ:]
        none = jnp.zeros_like(first)
        from_second = jnp.concatenate([second, none], axis=1)
        from_first = jnp.concatenate([none, first], axis=1)
        tall = jnp.concatenate([win, from_second, from_first], axis=0)
        y = jnp.dot(ky_ref[...], tall, preferred_element_type=jnp.float32)
        z = jnp.dot(y.astype(jnp.bfloat16), kz_ref[...], preferred_element_type=jnp.float32)
        for j in range(16):
            lane = pl.ds(pl.multiple_of((b * 16 + j) * LANES, LANES), LANES)
            out_ref[:, lane] = z[j * rows:(j + 1) * rows] + w_ref[:, lane].astype(jnp.float32)


def greet(neighbours):
    barrier = pltpu.get_barrier_semaphore()
    expected = 0
    for there, where in neighbours:
        if there is True:
            pl.semaphore_signal(barrier, inc=1, device_id=where, device_id_type=MESH)
            expected = expected + 1
        else:
            @pl.when(there)
            def _():
                pl.semaphore_signal(barrier, inc=1, device_id=where, device_id_type=MESH)
            expected = expected + there.astype(jnp.int32)
    pl.semaphore_wait(barrier, expected)


def slab_sides():
    me = lax.axis_index("gx")
    return (me > 0, {"gx": me - 1}), (me < lax.axis_size("gx") - 1, {"gx": me + 1})


def both_ways(to_left, to_right, from_left, from_right, send, recv):
    (has_left, left), (has_right, right) = slab_sides()
    leftward = pltpu.make_async_remote_copy(
        src_ref=to_left, dst_ref=from_right, send_sem=send.at[0], recv_sem=recv.at[0],
        device_id=left, device_id_type=MESH)
    rightward = pltpu.make_async_remote_copy(
        src_ref=to_right, dst_ref=from_left, send_sem=send.at[1], recv_sem=recv.at[1],
        device_id=right, device_id_type=MESH)
    pl.when(has_left)(leftward.start)
    pl.when(has_right)(rightward.start)

    def arrived():
        pl.when(has_left)(rightward.wait_recv)
        pl.when(has_right)(leftward.wait_recv)

        @pl.when(jnp.logical_not(has_left))
        def _():
            from_left[...] = jnp.zeros_like(from_left)

        @pl.when(jnp.logical_not(has_right))
        def _():
            from_right[...] = jnp.zeros_like(from_right)

    def sent():
        pl.when(has_left)(leftward.wait_send)
        pl.when(has_right)(rightward.wait_send)

    return arrived, sent


def cells_kernel(cell_ref, out_ref, left_ref, right_ref, send, recv):
    count = cell_ref.shape[1]
    greet(slab_sides())
    arrived, sent = both_ways(cell_ref, cell_ref, left_ref, right_ref, send, recv)
    out_ref[:, :count] = cell_ref[...]
    arrived()
    out_ref[:, count:2 * count] = left_ref[...]
    out_ref[:, 2 * count:] = right_ref[...]
    sent()


def residual_kernel(s_ref, pick_ref, innovation_ref, weight_ref, count_ref, out_ref,
                    to_left, to_right, s_left, s_right, share, peers, source, v_left, v_right,
                    s_send, s_recv, m_send, m_recv, v_send, v_recv):
    count = pick_ref.shape[1]
    members = lax.axis_size("mem")
    here = lax.axis_index("mem")
    others = [(True, {"mem": lax.rem(here + step, members)}) for step in range(1, members)]
    greet(list(slab_sides()) + others)

    to_left[...] = s_ref[:, count:2 * count]
    to_right[...] = s_ref[:, 2 * count:]
    arrived, s_sent = both_ways(to_left, to_right, s_left, s_right, s_send, s_recv)
    arrived()
    own = s_ref[:, :count] + s_left[...] + s_right[...]
    share[...] = pick_ref[...] * own

    copies = []
    for k, (_, where) in enumerate(others):
        copies.append(pltpu.make_async_remote_copy(
            src_ref=share, dst_ref=peers.at[k], send_sem=m_send.at[k], recv_sem=m_recv.at[k],
            device_id=where, device_id_type=MESH))
        copies[-1].start()
    sampled = share[...]
    for k, copy in enumerate(copies):
        copy.wait_recv()
        sampled = sampled + peers[k]
    live = lax.broadcasted_iota(jnp.int32, (1, count), 1) < count_ref[0]
    residual = jnp.where(live, weight_ref[...], 0.0) * (sampled - innovation_ref[...])
    source[...] = pick_ref[...] * residual

    arrived, v_sent = both_ways(source, source, v_left, v_right, v_send, v_recv)
    out_ref[:, :count] = source[...]
    arrived()
    out_ref[:, count:2 * count] = v_left[...]
    out_ref[:, 2 * count:] = v_right[...]
    s_sent()
    for copy in copies:
        copy.wait_send()
    v_sent()


def vmem(count):
    return [pl.BlockSpec(memory_space=pltpu.VMEM)] * count


def local(weights, perturbations, obs_cell, obs_slot, innovation, obs_weight, obs_count):
    rows, plane = weights.shape[1:]
    slots = perturbations.shape[0]
    count = obs_cell.shape[0]
    w = weights[0]
    pert = perturbations[:, 0]
    depth = LOW * rows
    wide = HIGH * LANES
    padded = (PAIRS + 16) * rows
    params = pltpu.CompilerParams(vmem_limit_bytes=VMEM_LIMIT)
    bf16 = jnp.bfloat16

    kz = jnp.asarray(z_band())
    ky_np = y_band(rows)
    ky, kyt = jnp.asarray(ky_np), jnp.asarray(np.ascontiguousarray(ky_np.T))
    kx = jnp.asarray(x_bands(rows))
    eye = jnp.asarray(np.eye(LANES).astype(ml_dtypes.bfloat16))

    cell = obs_cell.reshape(1, count)
    slot = obs_slot.reshape(1, count)
    cells = pl.pallas_call(
        cells_kernel,
        out_shape=jax.ShapeDtypeStruct((1, 3 * count), jnp.int32),
        in_specs=vmem(1),
        out_specs=vmem(1)[0],
        scratch_shapes=[pltpu.VMEM((1, count), jnp.int32)] * 2 + [pltpu.SemaphoreType.DMA((2,))] * 2,
        compiler_params=pltpu.CompilerParams(collective_id=0, has_side_effects=True),
        name="cells",
    )(cell)

    block = 2048
    picked = pl.pallas_call(
        functools.partial(pick_kernel, block),
        out_shape=jax.ShapeDtypeStruct((1, count), jnp.float32),
        in_specs=vmem(4),
        out_specs=vmem(1)[0],
        scratch_shapes=[
            pltpu.VMEM((slots * wide, depth), bf16),
            pltpu.VMEM((depth, block), bf16),
        ],
        compiler_params=params,
        cost_estimate=pl.CostEstimate(
            flops=2 * slots * rows * plane * count, bytes_accessed=4 * rows * plane,
            transcendentals=0),
        name="pick",
    )(pert, cell, slot, eye)

    sampled3 = pl.pallas_call(
        functools.partial(sample_kernel, block),
        out_shape=jax.ShapeDtypeStruct((1, 3 * count), jnp.float32),
        in_specs=vmem(5),
        out_specs=vmem(1)[0],
        scratch_shapes=[
            pltpu.VMEM((LANES, padded), bf16),
            pltpu.VMEM((wide, depth), bf16),
            pltpu.VMEM((depth, block), bf16),
        ],
        compiler_params=params,
        cost_estimate=pl.CostEstimate(
            flops=6 * rows * plane * count, bytes_accessed=2 * rows * plane, transcendentals=0),
        name="sample",
    )(w, cells, kz, kyt, kx)

    peers = lax.axis_size("mem") - 1
    line = pltpu.VMEM((1, count), jnp.float32)
    pair = pltpu.SemaphoreType.DMA((2,))
    each = pltpu.SemaphoreType.DMA((peers,))
    sources = pl.pallas_call(
        residual_kernel,
        out_shape=jax.ShapeDtypeStruct((1, 3 * count), jnp.float32),
        in_specs=vmem(4) + [pl.BlockSpec(memory_space=pltpu.SMEM)],
        out_specs=vmem(1)[0],
        scratch_shapes=[line] * 5 + [pltpu.VMEM((peers, 1, count), jnp.float32)] + [line] * 3
        + [pair, pair, each, each, pair, pair],
        compiler_params=pltpu.CompilerParams(collective_id=1, has_side_effects=True),
        name="residual",
    )(sampled3, picked, innovation.reshape(1, count), obs_weight.reshape(1, count), obs_count)

    back_block = 2048
    out = pl.pallas_call(
        functools.partial(back_kernel, back_block),
        out_shape=jax.ShapeDtypeStruct((rows, plane), jnp.float32),
        in_specs=vmem(6),
        out_specs=vmem(1)[0],
        scratch_shapes=[
            pltpu.VMEM((depth, wide), jnp.float32),
            pltpu.VMEM((padded, LANES), bf16),
            pltpu.VMEM((depth, back_block), bf16),
            pltpu.VMEM((wide, back_block), bf16),
        ],
        compiler_params=params,
        cost_estimate=pl.CostEstimate(
            flops=6 * rows * plane * count, bytes_accessed=6 * rows * plane, transcendentals=0),
        name="back",
    )(w, cells, sources, kz, ky, kx)
    return out[None]


def solution(mesh):
    return jax.shard_map(
        local,
        mesh=mesh,
        in_specs=(
            P("mem", "gx", None),
            P(None, "mem", "gx", None),
            P("gx"),
            P("gx"),
            P("gx"),
            P("gx"),
            P("gx"),
        ),
        out_specs=P("mem", "gx", None),
        check_vma=False,
    )
```

```python
import functools

import ml_dtypes
import numpy as np

import jax
import jax.numpy as jnp
from jax import lax
from jax.experimental import pallas as pl
from jax.experimental.pallas import tpu as pltpu
from jax.sharding import PartitionSpec as P

NY = 512
NZ = 64
REACH = 15
LANES = 128
PAIRS = NY // 2
LOW = 64
HIGH = PAIRS // LOW
UNROLL = 2
SUB = 512
VMEM_LIMIT = 56 * 1024 * 1024
NT = (((1,), (1,)), ((), ()))
MESH = pl.DeviceIdType.MESH


def tap_values():
    j = np.arange(-REACH, REACH + 1).astype(np.float32)
    bell = np.exp(-j * j / np.float32(98.0))
    return (bell / np.sqrt(np.sum(bell * bell))).astype(ml_dtypes.bfloat16)


def taps_at(offset):
    taps = tap_values()
    look = taps[np.clip(offset + REACH, 0, 2 * REACH)]
    return np.where(np.abs(offset) <= REACH, look, np.zeros_like(look))


def z_band():
    z = np.arange(LANES) % NZ
    half = np.arange(LANES) // NZ
    band = taps_at(z[:, None] - z[None, :])
    return np.where(half[:, None] == half[None, :], band, np.zeros_like(band))


def y_band(rows):
    out_c, out_x = np.arange(16 * rows) // rows, np.arange(16 * rows) % rows
    in_c, in_x = np.arange(32 * rows) // rows - 8, np.arange(32 * rows) % rows
    step = 2 * (in_c[None, :] - out_c[:, None])
    same = out_x[:, None] == in_x[None, :]
    parts = []
    for shift in (0, 1, -1):
        band = taps_at(step + shift)
        parts.append(np.where(same, band, np.zeros_like(band)))
    return np.concatenate(parts, axis=1)


def x_bands(rows):
    x = np.arange(rows)
    return np.stack([taps_at(x[:, None] - (x[None, :] + off)) for off in (0, -rows, rows)])


def split_cell(cell):
    x = cell >> 15
    pair = (cell >> 7) & (PAIRS - 1)
    low = pair & (LOW - 1)
    row = (pair // LOW) * LANES + (cell & (LANES - 1))
    return x, low, row


def fill_a(a_ref, x_rows, low, rows):
    count = x_rows.shape[1]
    low_b = jnp.broadcast_to(low.astype(jnp.float32), (rows, count)).astype(jnp.bfloat16)
    zero = jnp.zeros_like(x_rows)
    for c in range(LOW):
        a_ref[c * rows:(c + 1) * rows, :] = jnp.where(low_b == jnp.bfloat16(c), x_rows, zero)


def x_taps(kx, x, rows):
    hot = (lax.broadcasted_iota(jnp.int32, (rows, x.shape[1]), 0) == x)
    hot = hot.astype(jnp.float32).astype(jnp.bfloat16)
    if kx is None:
        return hot
    return jnp.dot(kx, hot, preferred_element_type=jnp.float32).astype(jnp.bfloat16)


def looked_up(table_ref, a_ref, x_rows, low, row, rows):
    found = []
    for j in range(0, x_rows.shape[1], SUB):
        part = slice(j, j + SUB)
        fill_a(a_ref.at[:, part], x_rows[:, part], low[:, part], rows)
        m = jnp.dot(table_ref[...], a_ref[:, part], preferred_element_type=jnp.float32)
        hit = lax.broadcasted_iota(jnp.int32, m.shape, 0) == row[:, part]
        found.append(jnp.sum(jnp.where(hit, m, 0.0), axis=0, keepdims=True))
    return jnp.concatenate(found, axis=1)


def pairs_block(w_ref, b, rows):
    parts = []
    for j in range(16):
        start = pl.multiple_of((b * 16 + j) * LANES, LANES)
        parts.append(w_ref[:, pl.ds(start, LANES)])
    return jnp.concatenate(parts, axis=0)


def sample_kernel(block, w_ref, cell_ref, kz_ref, kyt_ref, kx_ref, s_ref, z_ref, y_ref, a_ref):
    rows = w_ref.shape[0]
    span = 16 * rows
    pad = 8 * rows
    depth = LOW * rows
    z_ref[:, :pad] = jnp.zeros((LANES, pad), jnp.bfloat16)
    z_ref[:, pad + PAIRS * rows:] = jnp.zeros((LANES, pad), jnp.bfloat16)

    @pl.loop(0, PAIRS // 16, unroll=UNROLL)
    def _(b):
        part = pairs_block(w_ref, b, rows)
        z = lax.dot_general(kz_ref[...], part, NT, preferred_element_type=jnp.float32)
        z_ref[:, pl.ds(pl.multiple_of(pad + b * span, LANES), span)] = z.astype(jnp.bfloat16)

    @pl.loop(0, PAIRS // 16, unroll=UNROLL)
    def _(b):
        win = z_ref[:, pl.ds(pl.multiple_of(b * span, LANES), 2 * span)]
        top, bottom = win[:NZ], win[NZ:]
        none = jnp.zeros_like(top)
        from_bottom = jnp.concatenate([bottom, none], axis=0)
        from_top = jnp.concatenate([none, top], axis=0)
        wide = jnp.concatenate([win, from_bottom, from_top], axis=1)
        y = jnp.dot(wide, kyt_ref[...], preferred_element_type=jnp.float32)
        high = b // (LOW // 16)
        col = pl.multiple_of((b % (LOW // 16)) * span, LANES)
        y_ref[pl.ds(pl.multiple_of(high * LANES, LANES), LANES), pl.ds(col, span)] = y.astype(
            jnp.bfloat16)

    per_list = cell_ref.shape[1] // 3

    @pl.loop(0, cell_ref.shape[1] // block)
    def _(i):
        at = pl.ds(pl.multiple_of(i * block, block), block)
        x, low, row = split_cell(cell_ref[:, at])
        kx = kx_ref[i // (per_list // block)]
        s_ref[:, at] = looked_up(y_ref, a_ref, x_taps(kx, x, rows), low, row, rows)


def pick_kernel(block, p_ref, cell_ref, slot_ref, eye_ref, o_ref, t_ref, a_ref):
    slots, rows = p_ref.shape[:2]
    span = 16 * rows

    for t in range(slots):
        @pl.loop(0, PAIRS // 16, unroll=UNROLL)
        def _(b):
            part = pairs_block(p_ref.at[t], b, rows)
            z = lax.dot_general(eye_ref[...], part, NT, preferred_element_type=jnp.float32)
            high = b // (LOW // 16)
            col = pl.multiple_of((b % (LOW // 16)) * span, LANES)
            row0 = pl.multiple_of((t * HIGH + high) * LANES, LANES)
            t_ref[pl.ds(row0, LANES), pl.ds(col, span)] = z.astype(jnp.bfloat16)

    @pl.loop(0, cell_ref.shape[1] // block)
    def _(i):
        at = pl.ds(pl.multiple_of(i * block, block), block)
        x, low, row = split_cell(cell_ref[:, at])
        row = row + slot_ref[:, at] * (HIGH * LANES)
        o_ref[:, at] = looked_up(t_ref, a_ref, x_taps(None, x, rows), low, row, rows)


def back_kernel(block, w_ref, cell_ref, v_ref, kz_ref, ky_ref, kx_ref, out_ref,
                g_ref, x_ref, a_ref, b_ref):
    rows = w_ref.shape[0]
    span = 16 * rows
    pad = 8 * rows
    depth = LOW * rows
    per_list = cell_ref.shape[1] // 3
    g_ref[...] = jnp.zeros_like(g_ref)

    @pl.loop(0, cell_ref.shape[1] // block)
    def _(i):
        at = pl.ds(pl.multiple_of(i * block, block), block)
        x, low, row = split_cell(cell_ref[:, at])
        kx = kx_ref[i // (per_list // block)]
        fill_a(a_ref, x_taps(kx, x, rows), low, rows)
        shape = (HIGH * LANES, block)
        hit = lax.broadcasted_iota(jnp.int32, shape, 0) == row
        b_ref[...] = jnp.where(hit, v_ref[:, at], 0.0).astype(jnp.bfloat16)
        g_ref[...] += lax.dot_general(
            a_ref[...], b_ref[...], NT, preferred_element_type=jnp.float32)

    x_ref[:pad, :] = jnp.zeros((pad, LANES), jnp.bfloat16)
    x_ref[pad + PAIRS * rows:, :] = jnp.zeros((pad, LANES), jnp.bfloat16)
    for h in range(HIGH):
        x_ref[pad + h * depth:pad + (h + 1) * depth, :] = g_ref[
            :, h * LANES:(h + 1) * LANES].astype(jnp.bfloat16)

    @pl.loop(0, PAIRS // 16, unroll=UNROLL)
    def _(b):
        win = x_ref[pl.ds(pl.multiple_of(b * span, LANES), 2 * span), :]
        first, second = win[:, :NZ], win[:, NZ:]
        none = jnp.zeros_like(first)
        from_second = jnp.concatenate([second, none], axis=1)
        from_first = jnp.concatenate([none, first], axis=1)
        tall = jnp.concatenate([win, from_second, from_first], axis=0)
        y = jnp.dot(ky_ref[...], tall, preferred_element_type=jnp.float32)
        z = jnp.dot(y.astype(jnp.bfloat16), kz_ref[...], preferred_element_type=jnp.float32)
        for j in range(16):
            lane = pl.ds(pl.multiple_of((b * 16 + j) * LANES, LANES), LANES)
            out_ref[:, lane] = z[j * rows:(j + 1) * rows] + w_ref[:, lane].astype(jnp.float32)


def greet(neighbours):
    barrier = pltpu.get_barrier_semaphore()
    expected = 0
    for there, where in neighbours:
        if there is True:
            pl.semaphore_signal(barrier, inc=1, device_id=where, device_id_type=MESH)
            expected = expected + 1
        else:
            @pl.when(there)
            def _():
                pl.semaphore_signal(barrier, inc=1, device_id=where, device_id_type=MESH)
            expected = expected + there.astype(jnp.int32)
    pl.semaphore_wait(barrier, expected)


def slab_sides():
    me = lax.axis_index("gx")
    return (me > 0, {"gx": me - 1}), (me < lax.axis_size("gx") - 1, {"gx": me + 1})


def both_ways(to_left, to_right, from_left, from_right, send, recv):
    (has_left, left), (has_right, right) = slab_sides()
    leftward = pltpu.make_async_remote_copy(
        src_ref=to_left, dst_ref=from_right, send_sem=send.at[0], recv_sem=recv.at[0],
        device_id=left, device_id_type=MESH)
    rightward = pltpu.make_async_remote_copy(
        src_ref=to_right, dst_ref=from_left, send_sem=send.at[1], recv_sem=recv.at[1],
        device_id=right, device_id_type=MESH)
    pl.when(has_left)(leftward.start)
    pl.when(has_right)(rightward.start)

    def arrived():
        pl.when(has_left)(rightward.wait_recv)
        pl.when(has_right)(leftward.wait_recv)

        @pl.when(jnp.logical_not(has_left))
        def _():
            from_left[...] = jnp.zeros_like(from_left)

        @pl.when(jnp.logical_not(has_right))
        def _():
            from_right[...] = jnp.zeros_like(from_right)

    def sent():
        pl.when(has_left)(leftward.wait_send)
        pl.when(has_right)(rightward.wait_send)

    return arrived, sent


def cells_kernel(cell_ref, out_ref, left_ref, right_ref, send, recv):
    count = cell_ref.shape[1]
    greet(slab_sides())
    arrived, sent = both_ways(cell_ref, cell_ref, left_ref, right_ref, send, recv)
    out_ref[:, :count] = cell_ref[...]
    arrived()
    out_ref[:, count:2 * count] = left_ref[...]
    out_ref[:, 2 * count:] = right_ref[...]
    sent()


def residual_kernel(s_ref, pick_ref, innovation_ref, weight_ref, count_ref, out_ref,
                    to_left, to_right, s_left, s_right, share, peers, source, v_left, v_right,
                    s_send, s_recv, m_send, m_recv, v_send, v_recv):
    count = pick_ref.shape[1]
    members = lax.axis_size("mem")
    here = lax.axis_index("mem")
    others = [(True, {"mem": lax.rem(here + step, members)}) for step in range(1, members)]
    greet(list(slab_sides()) + others)

    to_left[...] = s_ref[:, count:2 * count]
    to_right[...] = s_ref[:, 2 * count:]
    arrived, s_sent = both_ways(to_left, to_right, s_left, s_right, s_send, s_recv)
    arrived()
    own = s_ref[:, :count] + s_left[...] + s_right[...]
    share[...] = pick_ref[...] * own

    copies = []
    for k, (_, where) in enumerate(others):
        copies.append(pltpu.make_async_remote_copy(
            src_ref=share, dst_ref=peers.at[k], send_sem=m_send.at[k], recv_sem=m_recv.at[k],
            device_id=where, device_id_type=MESH))
        copies[-1].start()
    sampled = share[...]
    for k, copy in enumerate(copies):
        copy.wait_recv()
        sampled = sampled + peers[k]
    live = lax.broadcasted_iota(jnp.int32, (1, count), 1) < count_ref[0]
    residual = jnp.where(live, weight_ref[...], 0.0) * (sampled - innovation_ref[...])
    source[...] = pick_ref[...] * residual

    arrived, v_sent = both_ways(source, source, v_left, v_right, v_send, v_recv)
    out_ref[:, :count] = source[...]
    arrived()
    out_ref[:, count:2 * count] = v_left[...]
    out_ref[:, 2 * count:] = v_right[...]
    s_sent()
    for copy in copies:
        copy.wait_send()
    v_sent()


def vmem(count):
    return [pl.BlockSpec(memory_space=pltpu.VMEM)] * count


def local(weights, perturbations, obs_cell, obs_slot, innovation, obs_weight, obs_count):
    rows, plane = weights.shape[1:]
    slots = perturbations.shape[0]
    count = obs_cell.shape[0]
    w = weights[0]
    pert = perturbations[:, 0]
    depth = LOW * rows
    wide = HIGH * LANES
    padded = (PAIRS + 16) * rows
    params = pltpu.CompilerParams(vmem_limit_bytes=VMEM_LIMIT)
    bf16 = jnp.bfloat16

    kz = jnp.asarray(z_band())
    ky_np = y_band(rows)
    ky, kyt = jnp.asarray(ky_np), jnp.asarray(np.ascontiguousarray(ky_np.T))
    kx = jnp.asarray(x_bands(rows))
    eye = jnp.asarray(np.eye(LANES).astype(ml_dtypes.bfloat16))

    cell = obs_cell.reshape(1, count)
    slot = obs_slot.reshape(1, count)
    cells = pl.pallas_call(
        cells_kernel,
        out_shape=jax.ShapeDtypeStruct((1, 3 * count), jnp.int32),
        in_specs=vmem(1),
        out_specs=vmem(1)[0],
        scratch_shapes=[pltpu.VMEM((1, count), jnp.int32)] * 2 + [pltpu.SemaphoreType.DMA((2,))] * 2,
        compiler_params=pltpu.CompilerParams(collective_id=0, has_side_effects=True),
        name="cells",
    )(cell)

    block = 2048
    picked = pl.pallas_call(
        functools.partial(pick_kernel, block),
        out_shape=jax.ShapeDtypeStruct((1, count), jnp.float32),
        in_specs=vmem(4),
        out_specs=vmem(1)[0],
        scratch_shapes=[
            pltpu.VMEM((slots * wide, depth), bf16),
            pltpu.VMEM((depth, block), bf16),
        ],
        compiler_params=params,
        cost_estimate=pl.CostEstimate(
            flops=2 * slots * rows * plane * count, bytes_accessed=4 * rows * plane,
            transcendentals=0),
        name="pick",
    )(pert, cell, slot, eye)

    sampled3 = pl.pallas_call(
        functools.partial(sample_kernel, block),
        out_shape=jax.ShapeDtypeStruct((1, 3 * count), jnp.float32),
        in_specs=vmem(5),
        out_specs=vmem(1)[0],
        scratch_shapes=[
            pltpu.VMEM((LANES, padded), bf16),
            pltpu.VMEM((wide, depth), bf16),
            pltpu.VMEM((depth, block), bf16),
        ],
        compiler_params=params,
        cost_estimate=pl.CostEstimate(
            flops=6 * rows * plane * count, bytes_accessed=2 * rows * plane, transcendentals=0),
        name="sample",
    )(w, cells, kz, kyt, kx)

    peers = lax.axis_size("mem") - 1
    line = pltpu.VMEM((1, count), jnp.float32)
    pair = pltpu.SemaphoreType.DMA((2,))
    each = pltpu.SemaphoreType.DMA((peers,))
    sources = pl.pallas_call(
        residual_kernel,
        out_shape=jax.ShapeDtypeStruct((1, 3 * count), jnp.float32),
        in_specs=vmem(4) + [pl.BlockSpec(memory_space=pltpu.SMEM)],
        out_specs=vmem(1)[0],
        scratch_shapes=[line] * 5 + [pltpu.VMEM((peers, 1, count), jnp.float32)] + [line] * 3
        + [pair, pair, each, each, pair, pair],
        compiler_params=pltpu.CompilerParams(collective_id=1, has_side_effects=True),
        name="residual",
    )(sampled3, picked, innovation.reshape(1, count), obs_weight.reshape(1, count), obs_count)

    back_block = 2048
    out = pl.pallas_call(
        functools.partial(back_kernel, back_block),
        out_shape=jax.ShapeDtypeStruct((rows, plane), jnp.float32),
        in_specs=vmem(6),
        out_specs=vmem(1)[0],
        scratch_shapes=[
            pltpu.VMEM((depth, wide), jnp.float32),
            pltpu.VMEM((padded, LANES), bf16),
            pltpu.VMEM((depth, back_block), bf16),
            pltpu.VMEM((wide, back_block), bf16),
        ],
        compiler_params=params,
        cost_estimate=pl.CostEstimate(
            flops=6 * rows * plane * count, bytes_accessed=6 * rows * plane, transcendentals=0),
        name="back",
    )(w, cells, sources, kz, ky, kx)
    return out[None]


def solution(mesh):
    return jax.shard_map(
        local,
        mesh=mesh,
        in_specs=(
            P("mem", "gx", None),
            P(None, "mem", "gx", None),
            P("gx"),
            P("gx"),
            P("gx"),
            P("gx"),
            P("gx"),
        ),
        out_specs=P("mem", "gx", None),
        check_vma=False,
    )
```

```python
import functools

import ml_dtypes
import numpy as np

import jax
import jax.numpy as jnp
from jax import lax
from jax.experimental import pallas as pl
from jax.experimental.pallas import tpu as pltpu
from jax.sharding import PartitionSpec as P

NY = 512
NZ = 64
REACH = 15
LANES = 128
PAIRS = NY // 2
LOW = 64
HIGH = PAIRS // LOW
UNROLL = 4
SUB = 512
BACK_SUB = 1024
VMEM_LIMIT = 56 * 1024 * 1024
NT = (((1,), (1,)), ((), ()))
MESH = pl.DeviceIdType.MESH


def tap_values():
    j = np.arange(-REACH, REACH + 1).astype(np.float32)
    bell = np.exp(-j * j / np.float32(98.0))
    return (bell / np.sqrt(np.sum(bell * bell))).astype(ml_dtypes.bfloat16)


def taps_at(offset):
    taps = tap_values()
    look = taps[np.clip(offset + REACH, 0, 2 * REACH)]
    return np.where(np.abs(offset) <= REACH, look, np.zeros_like(look))


def z_band():
    z = np.arange(LANES) % NZ
    half = np.arange(LANES) // NZ
    band = taps_at(z[:, None] - z[None, :])
    return np.where(half[:, None] == half[None, :], band, np.zeros_like(band))


def y_band(rows):
    out_c, out_x = np.arange(16 * rows) // rows, np.arange(16 * rows) % rows
    in_c, in_x = np.arange(32 * rows) // rows - 8, np.arange(32 * rows) % rows
    step = 2 * (in_c[None, :] - out_c[:, None])
    same = out_x[:, None] == in_x[None, :]
    parts = []
    for shift in (0, 1, -1):
        band = taps_at(step + shift)
        parts.append(np.where(same, band, np.zeros_like(band)))
    return np.concatenate(parts, axis=1)


def x_bands(rows):
    x = np.arange(rows)
    return np.stack([taps_at(x[:, None] - (x[None, :] + off)) for off in (0, -rows, rows)])


def split_cell(cell):
    x = cell >> 15
    pair = (cell >> 7) & (PAIRS - 1)
    low = pair & (LOW - 1)
    row = (pair // LOW) * LANES + (cell & (LANES - 1))
    return x, low, row


def fill_a(a_ref, x_rows, low, rows):
    count = x_rows.shape[1]
    low_b = jnp.broadcast_to(low.astype(jnp.float32), (rows, count)).astype(jnp.bfloat16)
    zero = jnp.zeros_like(x_rows)
    for c in range(LOW):
        a_ref[c * rows:(c + 1) * rows, :] = jnp.where(low_b == jnp.bfloat16(c), x_rows, zero)


def x_taps(kx, x, rows):
    hot = (lax.broadcasted_iota(jnp.int32, (rows, x.shape[1]), 0) == x)
    hot = hot.astype(jnp.float32).astype(jnp.bfloat16)
    if kx is None:
        return hot
    return jnp.dot(kx, hot, preferred_element_type=jnp.float32).astype(jnp.bfloat16)


def looked_up(table_ref, a_ref, x_rows, low, row, rows):
    found = []
    for j in range(0, x_rows.shape[1], SUB):
        part = slice(j, j + SUB)
        fill_a(a_ref.at[:, part], x_rows[:, part], low[:, part], rows)
        m = jnp.dot(table_ref[...], a_ref[:, part], preferred_element_type=jnp.float32)
        hit = lax.broadcasted_iota(jnp.int32, m.shape, 0) == row[:, part]
        found.append(jnp.sum(jnp.where(hit, m, 0.0), axis=0, keepdims=True))
    return jnp.concatenate(found, axis=1)


def pairs_block(w_ref, b, rows):
    parts = []
    for j in range(16):
        start = pl.multiple_of((b * 16 + j) * LANES, LANES)
        parts.append(w_ref[:, pl.ds(start, LANES)])
    return jnp.concatenate(parts, axis=0)


def sample_kernel(block, w_ref, cell_ref, kz_ref, kyt_ref, kx_ref, s_ref, z_ref, y_ref, a_ref):
    rows = w_ref.shape[0]
    span = 16 * rows
    pad = 8 * rows
    depth = LOW * rows
    z_ref[:, :pad] = jnp.zeros((LANES, pad), jnp.bfloat16)
    z_ref[:, pad + PAIRS * rows:] = jnp.zeros((LANES, pad), jnp.bfloat16)

    @pl.loop(0, PAIRS // 16, unroll=UNROLL)
    def _(b):
        part = pairs_block(w_ref, b, rows)
        z = lax.dot_general(kz_ref[...], part, NT, preferred_element_type=jnp.float32)
        z_ref[:, pl.ds(pl.multiple_of(pad + b * span, LANES), span)] = z.astype(jnp.bfloat16)

    @pl.loop(0, PAIRS // 16, unroll=UNROLL)
    def _(b):
        win = z_ref[:, pl.ds(pl.multiple_of(b * span, LANES), 2 * span)]
        top, bottom = win[:NZ], win[NZ:]
        none = jnp.zeros_like(top)
        from_bottom = jnp.concatenate([bottom, none], axis=0)
        from_top = jnp.concatenate([none, top], axis=0)
        wide = jnp.concatenate([win, from_bottom, from_top], axis=1)
        y = jnp.dot(wide, kyt_ref[...], preferred_element_type=jnp.float32)
        high = b // (LOW // 16)
        col = pl.multiple_of((b % (LOW // 16)) * span, LANES)
        y_ref[pl.ds(pl.multiple_of(high * LANES, LANES), LANES), pl.ds(col, span)] = y.astype(
            jnp.bfloat16)

    per_list = cell_ref.shape[1] // 3

    @pl.loop(0, cell_ref.shape[1] // block)
    def _(i):
        at = pl.ds(pl.multiple_of(i * block, block), block)
        x, low, row = split_cell(cell_ref[:, at])
        kx = kx_ref[i // (per_list // block)]
        s_ref[:, at] = looked_up(y_ref, a_ref, x_taps(kx, x, rows), low, row, rows)


def pick_kernel(block, p_ref, cell_ref, slot_ref, eye_ref, o_ref, t_ref, a_ref):
    slots, rows = p_ref.shape[:2]
    span = 16 * rows

    for t in range(slots):
        @pl.loop(0, PAIRS // 16, unroll=UNROLL)
        def _(b):
            part = pairs_block(p_ref.at[t], b, rows)
            z = lax.dot_general(eye_ref[...], part, NT, preferred_element_type=jnp.float32)
            high = b // (LOW // 16)
            col = pl.multiple_of((b % (LOW // 16)) * span, LANES)
            row0 = pl.multiple_of((t * HIGH + high) * LANES, LANES)
            t_ref[pl.ds(row0, LANES), pl.ds(col, span)] = z.astype(jnp.bfloat16)

    @pl.loop(0, cell_ref.shape[1] // block)
    def _(i):
        at = pl.ds(pl.multiple_of(i * block, block), block)
        x, low, row = split_cell(cell_ref[:, at])
        row = row + slot_ref[:, at] * (HIGH * LANES)
        o_ref[:, at] = looked_up(t_ref, a_ref, x_taps(None, x, rows), low, row, rows)


def back_kernel(block, w_ref, cell_ref, v_ref, kz_ref, ky_ref, kx_ref, out_ref,
                g_ref, x_ref, a_ref, b_ref):
    rows = w_ref.shape[0]
    span = 16 * rows
    pad = 8 * rows
    depth = LOW * rows
    per_list = cell_ref.shape[1] // 3
    g_ref[...] = jnp.zeros_like(g_ref)

    @pl.loop(0, cell_ref.shape[1] // block)
    def _(i):
        at = pl.ds(pl.multiple_of(i * block, block), block)
        x, low, row = split_cell(cell_ref[:, at])
        kx = kx_ref[i // (per_list // block)]
        x_rows, value = x_taps(kx, x, rows), v_ref[:, at]
        total = g_ref[...]
        for j in range(0, block, BACK_SUB):
            part = slice(j, j + BACK_SUB)
            fill_a(a_ref.at[:, part], x_rows[:, part], low[:, part], rows)
            hit = lax.broadcasted_iota(jnp.int32, (HIGH * LANES, BACK_SUB), 0) == row[:, part]
            b_ref[:, part] = jnp.where(hit, value[:, part], 0.0).astype(jnp.bfloat16)
            total = total + lax.dot_general(
                a_ref[:, part], b_ref[:, part], NT, preferred_element_type=jnp.float32)
        g_ref[...] = total

    x_ref[:pad, :] = jnp.zeros((pad, LANES), jnp.bfloat16)
    x_ref[pad + PAIRS * rows:, :] = jnp.zeros((pad, LANES), jnp.bfloat16)
    for h in range(HIGH):
        x_ref[pad + h * depth:pad + (h + 1) * depth, :] = g_ref[
            :, h * LANES:(h + 1) * LANES].astype(jnp.bfloat16)

    @pl.loop(0, PAIRS // 16, unroll=UNROLL)
    def _(b):
        win = x_ref[pl.ds(pl.multiple_of(b * span, LANES), 2 * span), :]
        first, second = win[:, :NZ], win[:, NZ:]
        none = jnp.zeros_like(first)
        from_second = jnp.concatenate([second, none], axis=1)
        from_first = jnp.concatenate([none, first], axis=1)
        tall = jnp.concatenate([win, from_second, from_first], axis=0)
        y = jnp.dot(ky_ref[...], tall, preferred_element_type=jnp.float32)
        z = jnp.dot(y.astype(jnp.bfloat16), kz_ref[...], preferred_element_type=jnp.float32)
        for j in range(16):
            lane = pl.ds(pl.multiple_of((b * 16 + j) * LANES, LANES), LANES)
            out_ref[:, lane] = z[j * rows:(j + 1) * rows] + w_ref[:, lane].astype(jnp.float32)


def greet(neighbours):
    barrier = pltpu.get_barrier_semaphore()
    expected = 0
    for there, where in neighbours:
        if there is True:
            pl.semaphore_signal(barrier, inc=1, device_id=where, device_id_type=MESH)
            expected = expected + 1
        else:
            @pl.when(there)
            def _():
                pl.semaphore_signal(barrier, inc=1, device_id=where, device_id_type=MESH)
            expected = expected + there.astype(jnp.int32)
    pl.semaphore_wait(barrier, expected)


def slab_sides():
    me = lax.axis_index("gx")
    return (me > 0, {"gx": me - 1}), (me < lax.axis_size("gx") - 1, {"gx": me + 1})


def both_ways(to_left, to_right, from_left, from_right, send, recv):
    (has_left, left), (has_right, right) = slab_sides()
    leftward = pltpu.make_async_remote_copy(
        src_ref=to_left, dst_ref=from_right, send_sem=send.at[0], recv_sem=recv.at[0],
        device_id=left, device_id_type=MESH)
    rightward = pltpu.make_async_remote_copy(
        src_ref=to_right, dst_ref=from_left, send_sem=send.at[1], recv_sem=recv.at[1],
        device_id=right, device_id_type=MESH)
    pl.when(has_left)(leftward.start)
    pl.when(has_right)(rightward.start)

    def arrived():
        pl.when(has_left)(rightward.wait_recv)
        pl.when(has_right)(leftward.wait_recv)

        @pl.when(jnp.logical_not(has_left))
        def _():
            from_left[...] = jnp.zeros_like(from_left)

        @pl.when(jnp.logical_not(has_right))
        def _():
            from_right[...] = jnp.zeros_like(from_right)

    def sent():
        pl.when(has_left)(leftward.wait_send)
        pl.when(has_right)(rightward.wait_send)

    return arrived, sent


def cells_kernel(cell_ref, out_ref, left_ref, right_ref, send, recv):
    count = cell_ref.shape[1]
    greet(slab_sides())
    arrived, sent = both_ways(cell_ref, cell_ref, left_ref, right_ref, send, recv)
    out_ref[:, :count] = cell_ref[...]
    arrived()
    out_ref[:, count:2 * count] = left_ref[...]
    out_ref[:, 2 * count:] = right_ref[...]
    sent()


def residual_kernel(s_ref, pick_ref, innovation_ref, weight_ref, count_ref, out_ref,
                    to_left, to_right, s_left, s_right, share, peers, source, v_left, v_right,
                    s_send, s_recv, m_send, m_recv, v_send, v_recv):
    count = pick_ref.shape[1]
    members = lax.axis_size("mem")
    here = lax.axis_index("mem")
    others = [(True, {"mem": lax.rem(here + step, members)}) for step in range(1, members)]
    greet(list(slab_sides()) + others)

    to_left[...] = s_ref[:, count:2 * count]
    to_right[...] = s_ref[:, 2 * count:]
    arrived, s_sent = both_ways(to_left, to_right, s_left, s_right, s_send, s_recv)
    arrived()
    own = s_ref[:, :count] + s_left[...] + s_right[...]
    share[...] = pick_ref[...] * own

    copies = []
    for k, (_, where) in enumerate(others):
        copies.append(pltpu.make_async_remote_copy(
            src_ref=share, dst_ref=peers.at[k], send_sem=m_send.at[k], recv_sem=m_recv.at[k],
            device_id=where, device_id_type=MESH))
        copies[-1].start()
    sampled = share[...]
    for k, copy in enumerate(copies):
        copy.wait_recv()
        sampled = sampled + peers[k]
    live = lax.broadcasted_iota(jnp.int32, (1, count), 1) < count_ref[0]
    residual = jnp.where(live, weight_ref[...], 0.0) * (sampled - innovation_ref[...])
    source[...] = pick_ref[...] * residual

    arrived, v_sent = both_ways(source, source, v_left, v_right, v_send, v_recv)
    out_ref[:, :count] = source[...]
    arrived()
    out_ref[:, count:2 * count] = v_left[...]
    out_ref[:, 2 * count:] = v_right[...]
    s_sent()
    for copy in copies:
        copy.wait_send()
    v_sent()


def vmem(count):
    return [pl.BlockSpec(memory_space=pltpu.VMEM)] * count


def local(weights, perturbations, obs_cell, obs_slot, innovation, obs_weight, obs_count):
    rows, plane = weights.shape[1:]
    slots = perturbations.shape[0]
    count = obs_cell.shape[0]
    w = weights[0]
    pert = perturbations[:, 0]
    depth = LOW * rows
    wide = HIGH * LANES
    padded = (PAIRS + 16) * rows
    params = pltpu.CompilerParams(vmem_limit_bytes=VMEM_LIMIT)
    bf16 = jnp.bfloat16

    kz = jnp.asarray(z_band())
    ky_np = y_band(rows)
    ky, kyt = jnp.asarray(ky_np), jnp.asarray(np.ascontiguousarray(ky_np.T))
    kx = jnp.asarray(x_bands(rows))
    eye = jnp.asarray(np.eye(LANES).astype(ml_dtypes.bfloat16))

    cell = obs_cell.reshape(1, count)
    slot = obs_slot.reshape(1, count)
    cells = pl.pallas_call(
        cells_kernel,
        out_shape=jax.ShapeDtypeStruct((1, 3 * count), jnp.int32),
        in_specs=vmem(1),
        out_specs=vmem(1)[0],
        scratch_shapes=[pltpu.VMEM((1, count), jnp.int32)] * 2 + [pltpu.SemaphoreType.DMA((2,))] * 2,
        compiler_params=pltpu.CompilerParams(collective_id=0, has_side_effects=True),
        name="cells",
    )(cell)

    block = 2048
    picked = pl.pallas_call(
        functools.partial(pick_kernel, block),
        out_shape=jax.ShapeDtypeStruct((1, count), jnp.float32),
        in_specs=vmem(4),
        out_specs=vmem(1)[0],
        scratch_shapes=[
            pltpu.VMEM((slots * wide, depth), bf16),
            pltpu.VMEM((depth, block), bf16),
        ],
        compiler_params=params,
        cost_estimate=pl.CostEstimate(
            flops=2 * slots * rows * plane * count, bytes_accessed=4 * rows * plane,
            transcendentals=0),
        name="pick",
    )(pert, cell, slot, eye)

    sampled3 = pl.pallas_call(
        functools.partial(sample_kernel, block),
        out_shape=jax.ShapeDtypeStruct((1, 3 * count), jnp.float32),
        in_specs=vmem(5),
        out_specs=vmem(1)[0],
        scratch_shapes=[
            pltpu.VMEM((LANES, padded), bf16),
            pltpu.VMEM((wide, depth), bf16),
            pltpu.VMEM((depth, block), bf16),
        ],
        compiler_params=params,
        cost_estimate=pl.CostEstimate(
            flops=6 * rows * plane * count, bytes_accessed=2 * rows * plane, transcendentals=0),
        name="sample",
    )(w, cells, kz, kyt, kx)

    peers = lax.axis_size("mem") - 1
    line = pltpu.VMEM((1, count), jnp.float32)
    pair = pltpu.SemaphoreType.DMA((2,))
    each = pltpu.SemaphoreType.DMA((peers,))
    sources = pl.pallas_call(
        residual_kernel,
        out_shape=jax.ShapeDtypeStruct((1, 3 * count), jnp.float32),
        in_specs=vmem(4) + [pl.BlockSpec(memory_space=pltpu.SMEM)],
        out_specs=vmem(1)[0],
        scratch_shapes=[line] * 5 + [pltpu.VMEM((peers, 1, count), jnp.float32)] + [line] * 3
        + [pair, pair, each, each, pair, pair],
        compiler_params=pltpu.CompilerParams(collective_id=1, has_side_effects=True),
        name="residual",
    )(sampled3, picked, innovation.reshape(1, count), obs_weight.reshape(1, count), obs_count)

    back_block = 2048
    out = pl.pallas_call(
        functools.partial(back_kernel, back_block),
        out_shape=jax.ShapeDtypeStruct((rows, plane), jnp.float32),
        in_specs=vmem(6),
        out_specs=vmem(1)[0],
        scratch_shapes=[
            pltpu.VMEM((depth, wide), jnp.float32),
            pltpu.VMEM((padded, LANES), bf16),
            pltpu.VMEM((depth, back_block), bf16),
            pltpu.VMEM((wide, back_block), bf16),
        ],
        compiler_params=params,
        cost_estimate=pl.CostEstimate(
            flops=6 * rows * plane * count, bytes_accessed=6 * rows * plane, transcendentals=0),
        name="back",
    )(w, cells, sources, kz, ky, kx)
    return out[None]


def solution(mesh):
    return jax.shard_map(
        local,
        mesh=mesh,
        in_specs=(
            P("mem", "gx", None),
            P(None, "mem", "gx", None),
            P("gx"),
            P("gx"),
            P("gx"),
            P("gx"),
            P("gx"),
        ),
        out_specs=P("mem", "gx", None),
        check_vma=False,
    )
```

```python
import functools

import ml_dtypes
import numpy as np

import jax
import jax.numpy as jnp
from jax import lax
from jax.experimental import pallas as pl
from jax.experimental.pallas import tpu as pltpu
from jax.sharding import PartitionSpec as P

NY = 512
NZ = 64
REACH = 15
LANES = 128
PAIRS = NY // 2
LOW = 64
HIGH = PAIRS // LOW
UNROLL = 8
SUB = 512
BACK_SUB = 1024
VMEM_LIMIT = 56 * 1024 * 1024
NT = (((1,), (1,)), ((), ()))
MESH = pl.DeviceIdType.MESH


def tap_values():
    j = np.arange(-REACH, REACH + 1).astype(np.float32)
    bell = np.exp(-j * j / np.float32(98.0))
    return (bell / np.sqrt(np.sum(bell * bell))).astype(ml_dtypes.bfloat16)


def taps_at(offset):
    taps = tap_values()
    look = taps[np.clip(offset + REACH, 0, 2 * REACH)]
    return np.where(np.abs(offset) <= REACH, look, np.zeros_like(look))


def z_band():
    z = np.arange(LANES) % NZ
    half = np.arange(LANES) // NZ
    band = taps_at(z[:, None] - z[None, :])
    return np.where(half[:, None] == half[None, :], band, np.zeros_like(band))


def y_band(rows):
    out_c, out_x = np.arange(16 * rows) // rows, np.arange(16 * rows) % rows
    in_c, in_x = np.arange(32 * rows) // rows - 8, np.arange(32 * rows) % rows
    step = 2 * (in_c[None, :] - out_c[:, None])
    same = out_x[:, None] == in_x[None, :]
    parts = []
    for shift in (0, 1, -1):
        band = taps_at(step + shift)
        parts.append(np.where(same, band, np.zeros_like(band)))
    return np.concatenate(parts, axis=1)


def x_bands(rows):
    x = np.arange(rows)
    return np.stack([taps_at(x[:, None] - (x[None, :] + off)) for off in (0, -rows, rows)])


def split_cell(cell):
    x = cell >> 15
    pair = (cell >> 7) & (PAIRS - 1)
    low = pair & (LOW - 1)
    row = (pair // LOW) * LANES + (cell & (LANES - 1))
    return x, low, row


def fill_a(a_ref, x_rows, low, rows):
    count = x_rows.shape[1]
    low_b = jnp.broadcast_to(low.astype(jnp.float32), (rows, count)).astype(jnp.bfloat16)
    zero = jnp.zeros_like(x_rows)
    for c in range(LOW):
        a_ref[c * rows:(c + 1) * rows, :] = jnp.where(low_b == jnp.bfloat16(c), x_rows, zero)


def x_taps(kx, x, rows):
    hot = (lax.broadcasted_iota(jnp.int32, (rows, x.shape[1]), 0) == x)
    hot = hot.astype(jnp.float32).astype(jnp.bfloat16)
    if kx is None:
        return hot
    return jnp.dot(kx, hot, preferred_element_type=jnp.float32).astype(jnp.bfloat16)


def looked_up(table_ref, a_ref, x_rows, low, row, rows):
    found = []
    for j in range(0, x_rows.shape[1], SUB):
        part = slice(j, j + SUB)
        fill_a(a_ref.at[:, part], x_rows[:, part], low[:, part], rows)
        m = jnp.dot(table_ref[...], a_ref[:, part], preferred_element_type=jnp.float32)
        hit = lax.broadcasted_iota(jnp.int32, m.shape, 0) == row[:, part]
        found.append(jnp.sum(jnp.where(hit, m, 0.0), axis=0, keepdims=True))
    return jnp.concatenate(found, axis=1)


def pairs_block(w_ref, b, rows):
    parts = []
    for j in range(16):
        start = pl.multiple_of((b * 16 + j) * LANES, LANES)
        parts.append(w_ref[:, pl.ds(start, LANES)])
    return jnp.concatenate(parts, axis=0)


def sample_kernel(block, w_ref, cell_ref, kz_ref, kyt_ref, kx_ref, s_ref, z_ref, y_ref, a_ref):
    rows = w_ref.shape[0]
    span = 16 * rows
    pad = 8 * rows
    depth = LOW * rows
    z_ref[:, :pad] = jnp.zeros((LANES, pad), jnp.bfloat16)
    z_ref[:, pad + PAIRS * rows:] = jnp.zeros((LANES, pad), jnp.bfloat16)

    @pl.loop(0, PAIRS // 16, unroll=UNROLL)
    def _(b):
        part = pairs_block(w_ref, b, rows)
        z = lax.dot_general(kz_ref[...], part, NT, preferred_element_type=jnp.float32)
        z_ref[:, pl.ds(pl.multiple_of(pad + b * span, LANES), span)] = z.astype(jnp.bfloat16)

    @pl.loop(0, PAIRS // 16, unroll=UNROLL)
    def _(b):
        win = z_ref[:, pl.ds(pl.multiple_of(b * span, LANES), 2 * span)]
        top, bottom = win[:NZ], win[NZ:]
        none = jnp.zeros_like(top)
        from_bottom = jnp.concatenate([bottom, none], axis=0)
        from_top = jnp.concatenate([none, top], axis=0)
        wide = jnp.concatenate([win, from_bottom, from_top], axis=1)
        y = jnp.dot(wide, kyt_ref[...], preferred_element_type=jnp.float32)
        high = b // (LOW // 16)
        col = pl.multiple_of((b % (LOW // 16)) * span, LANES)
        y_ref[pl.ds(pl.multiple_of(high * LANES, LANES), LANES), pl.ds(col, span)] = y.astype(
            jnp.bfloat16)

    per_list = cell_ref.shape[1] // 3

    @pl.loop(0, cell_ref.shape[1] // block)
    def _(i):
        at = pl.ds(pl.multiple_of(i * block, block), block)
        x, low, row = split_cell(cell_ref[:, at])
        kx = kx_ref[i // (per_list // block)]
        s_ref[:, at] = looked_up(y_ref, a_ref, x_taps(kx, x, rows), low, row, rows)


def pick_kernel(block, p_ref, cell_ref, slot_ref, eye_ref, o_ref, t_ref, a_ref):
    slots, rows = p_ref.shape[:2]
    span = 16 * rows

    for t in range(slots):
        @pl.loop(0, PAIRS // 16, unroll=UNROLL)
        def _(b):
            part = pairs_block(p_ref.at[t], b, rows)
            z = lax.dot_general(eye_ref[...], part, NT, preferred_element_type=jnp.float32)
            high = b // (LOW // 16)
            col = pl.multiple_of((b % (LOW // 16)) * span, LANES)
            row0 = pl.multiple_of((t * HIGH + high) * LANES, LANES)
            t_ref[pl.ds(row0, LANES), pl.ds(col, span)] = z.astype(jnp.bfloat16)

    @pl.loop(0, cell_ref.shape[1] // block)
    def _(i):
        at = pl.ds(pl.multiple_of(i * block, block), block)
        x, low, row = split_cell(cell_ref[:, at])
        row = row + slot_ref[:, at] * (HIGH * LANES)
        o_ref[:, at] = looked_up(t_ref, a_ref, x_taps(None, x, rows), low, row, rows)


def back_kernel(block, w_ref, cell_ref, v_ref, kz_ref, ky_ref, kx_ref, out_ref,
                g_ref, x_ref, a_ref, b_ref):
    rows = w_ref.shape[0]
    span = 16 * rows
    pad = 8 * rows
    depth = LOW * rows
    per_list = cell_ref.shape[1] // 3
    g_ref[...] = jnp.zeros_like(g_ref)

    @pl.loop(0, cell_ref.shape[1] // block)
    def _(i):
        at = pl.ds(pl.multiple_of(i * block, block), block)
        x, low, row = split_cell(cell_ref[:, at])
        kx = kx_ref[i // (per_list // block)]
        x_rows, value = x_taps(kx, x, rows), v_ref[:, at]
        total = g_ref[...]
        for j in range(0, block, BACK_SUB):
            part = slice(j, j + BACK_SUB)
            fill_a(a_ref.at[:, part], x_rows[:, part], low[:, part], rows)
            hit = lax.broadcasted_iota(jnp.int32, (HIGH * LANES, BACK_SUB), 0) == row[:, part]
            b_ref[:, part] = jnp.where(hit, value[:, part], 0.0).astype(jnp.bfloat16)
            total = total + lax.dot_general(
                a_ref[:, part], b_ref[:, part], NT, preferred_element_type=jnp.float32)
        g_ref[...] = total

    x_ref[:pad, :] = jnp.zeros((pad, LANES), jnp.bfloat16)
    x_ref[pad + PAIRS * rows:, :] = jnp.zeros((pad, LANES), jnp.bfloat16)
    for h in range(HIGH):
        x_ref[pad + h * depth:pad + (h + 1) * depth, :] = g_ref[
            :, h * LANES:(h + 1) * LANES].astype(jnp.bfloat16)

    @pl.loop(0, PAIRS // 16, unroll=UNROLL)
    def _(b):
        win = x_ref[pl.ds(pl.multiple_of(b * span, LANES), 2 * span), :]
        first, second = win[:, :NZ], win[:, NZ:]
        none = jnp.zeros_like(first)
        from_second = jnp.concatenate([second, none], axis=1)
        from_first = jnp.concatenate([none, first], axis=1)
        tall = jnp.concatenate([win, from_second, from_first], axis=0)
        y = jnp.dot(ky_ref[...], tall, preferred_element_type=jnp.float32)
        z = jnp.dot(y.astype(jnp.bfloat16), kz_ref[...], preferred_element_type=jnp.float32)
        for j in range(16):
            lane = pl.ds(pl.multiple_of((b * 16 + j) * LANES, LANES), LANES)
            out_ref[:, lane] = z[j * rows:(j + 1) * rows] + w_ref[:, lane].astype(jnp.float32)


def greet(neighbours):
    barrier = pltpu.get_barrier_semaphore()
    expected = 0
    for there, where in neighbours:
        if there is True:
            pl.semaphore_signal(barrier, inc=1, device_id=where, device_id_type=MESH)
            expected = expected + 1
        else:
            @pl.when(there)
            def _():
                pl.semaphore_signal(barrier, inc=1, device_id=where, device_id_type=MESH)
            expected = expected + there.astype(jnp.int32)
    pl.semaphore_wait(barrier, expected)


def slab_sides():
    me = lax.axis_index("gx")
    return (me > 0, {"gx": me - 1}), (me < lax.axis_size("gx") - 1, {"gx": me + 1})


def both_ways(to_left, to_right, from_left, from_right, send, recv):
    (has_left, left), (has_right, right) = slab_sides()
    leftward = pltpu.make_async_remote_copy(
        src_ref=to_left, dst_ref=from_right, send_sem=send.at[0], recv_sem=recv.at[0],
        device_id=left, device_id_type=MESH)
    rightward = pltpu.make_async_remote_copy(
        src_ref=to_right, dst_ref=from_left, send_sem=send.at[1], recv_sem=recv.at[1],
        device_id=right, device_id_type=MESH)
    pl.when(has_left)(leftward.start)
    pl.when(has_right)(rightward.start)

    def arrived():
        pl.when(has_left)(rightward.wait_recv)
        pl.when(has_right)(leftward.wait_recv)

        @pl.when(jnp.logical_not(has_left))
        def _():
            from_left[...] = jnp.zeros_like(from_left)

        @pl.when(jnp.logical_not(has_right))
        def _():
            from_right[...] = jnp.zeros_like(from_right)

    def sent():
        pl.when(has_left)(leftward.wait_send)
        pl.when(has_right)(rightward.wait_send)

    return arrived, sent


def cells_kernel(cell_ref, out_ref, left_ref, right_ref, send, recv):
    count = cell_ref.shape[1]
    greet(slab_sides())
    arrived, sent = both_ways(cell_ref, cell_ref, left_ref, right_ref, send, recv)
    out_ref[:, :count] = cell_ref[...]
    arrived()
    out_ref[:, count:2 * count] = left_ref[...]
    out_ref[:, 2 * count:] = right_ref[...]
    sent()


def residual_kernel(s_ref, pick_ref, innovation_ref, weight_ref, count_ref, out_ref,
                    to_left, to_right, s_left, s_right, share, peers, source, v_left, v_right,
                    s_send, s_recv, m_send, m_recv, v_send, v_recv):
    count = pick_ref.shape[1]
    members = lax.axis_size("mem")
    here = lax.axis_index("mem")
    others = [(True, {"mem": lax.rem(here + step, members)}) for step in range(1, members)]
    greet(list(slab_sides()) + others)

    to_left[...] = s_ref[:, count:2 * count]
    to_right[...] = s_ref[:, 2 * count:]
    arrived, s_sent = both_ways(to_left, to_right, s_left, s_right, s_send, s_recv)
    arrived()
    own = s_ref[:, :count] + s_left[...] + s_right[...]
    share[...] = pick_ref[...] * own

    copies = []
    for k, (_, where) in enumerate(others):
        copies.append(pltpu.make_async_remote_copy(
            src_ref=share, dst_ref=peers.at[k], send_sem=m_send.at[k], recv_sem=m_recv.at[k],
            device_id=where, device_id_type=MESH))
        copies[-1].start()
    sampled = share[...]
    for k, copy in enumerate(copies):
        copy.wait_recv()
        sampled = sampled + peers[k]
    live = lax.broadcasted_iota(jnp.int32, (1, count), 1) < count_ref[0]
    residual = jnp.where(live, weight_ref[...], 0.0) * (sampled - innovation_ref[...])
    source[...] = pick_ref[...] * residual

    arrived, v_sent = both_ways(source, source, v_left, v_right, v_send, v_recv)
    out_ref[:, :count] = source[...]
    arrived()
    out_ref[:, count:2 * count] = v_left[...]
    out_ref[:, 2 * count:] = v_right[...]
    s_sent()
    for copy in copies:
        copy.wait_send()
    v_sent()


def vmem(count):
    return [pl.BlockSpec(memory_space=pltpu.VMEM)] * count


def local(weights, perturbations, obs_cell, obs_slot, innovation, obs_weight, obs_count):
    rows, plane = weights.shape[1:]
    slots = perturbations.shape[0]
    count = obs_cell.shape[0]
    w = weights[0]
    pert = perturbations[:, 0]
    depth = LOW * rows
    wide = HIGH * LANES
    padded = (PAIRS + 16) * rows
    params = pltpu.CompilerParams(vmem_limit_bytes=VMEM_LIMIT)
    bf16 = jnp.bfloat16

    kz = jnp.asarray(z_band())
    ky_np = y_band(rows)
    ky, kyt = jnp.asarray(ky_np), jnp.asarray(np.ascontiguousarray(ky_np.T))
    kx = jnp.asarray(x_bands(rows))
    eye = jnp.asarray(np.eye(LANES).astype(ml_dtypes.bfloat16))

    cell = obs_cell.reshape(1, count)
    slot = obs_slot.reshape(1, count)
    cells = pl.pallas_call(
        cells_kernel,
        out_shape=jax.ShapeDtypeStruct((1, 3 * count), jnp.int32),
        in_specs=vmem(1),
        out_specs=vmem(1)[0],
        scratch_shapes=[pltpu.VMEM((1, count), jnp.int32)] * 2 + [pltpu.SemaphoreType.DMA((2,))] * 2,
        compiler_params=pltpu.CompilerParams(collective_id=0, has_side_effects=True),
        name="cells",
    )(cell)

    block = 2048
    picked = pl.pallas_call(
        functools.partial(pick_kernel, block),
        out_shape=jax.ShapeDtypeStruct((1, count), jnp.float32),
        in_specs=vmem(4),
        out_specs=vmem(1)[0],
        scratch_shapes=[
            pltpu.VMEM((slots * wide, depth), bf16),
            pltpu.VMEM((depth, block), bf16),
        ],
        compiler_params=params,
        cost_estimate=pl.CostEstimate(
            flops=2 * slots * rows * plane * count, bytes_accessed=4 * rows * plane,
            transcendentals=0),
        name="pick",
    )(pert, cell, slot, eye)

    sampled3 = pl.pallas_call(
        functools.partial(sample_kernel, block),
        out_shape=jax.ShapeDtypeStruct((1, 3 * count), jnp.float32),
        in_specs=vmem(5),
        out_specs=vmem(1)[0],
        scratch_shapes=[
            pltpu.VMEM((LANES, padded), bf16),
            pltpu.VMEM((wide, depth), bf16),
            pltpu.VMEM((depth, block), bf16),
        ],
        compiler_params=params,
        cost_estimate=pl.CostEstimate(
            flops=6 * rows * plane * count, bytes_accessed=2 * rows * plane, transcendentals=0),
        name="sample",
    )(w, cells, kz, kyt, kx)

    peers = lax.axis_size("mem") - 1
    line = pltpu.VMEM((1, count), jnp.float32)
    pair = pltpu.SemaphoreType.DMA((2,))
    each = pltpu.SemaphoreType.DMA((peers,))
    sources = pl.pallas_call(
        residual_kernel,
        out_shape=jax.ShapeDtypeStruct((1, 3 * count), jnp.float32),
        in_specs=vmem(4) + [pl.BlockSpec(memory_space=pltpu.SMEM)],
        out_specs=vmem(1)[0],
        scratch_shapes=[line] * 5 + [pltpu.VMEM((peers, 1, count), jnp.float32)] + [line] * 3
        + [pair, pair, each, each, pair, pair],
        compiler_params=pltpu.CompilerParams(collective_id=1, has_side_effects=True),
        name="residual",
    )(sampled3, picked, innovation.reshape(1, count), obs_weight.reshape(1, count), obs_count)

    back_block = 2048
    out = pl.pallas_call(
        functools.partial(back_kernel, back_block),
        out_shape=jax.ShapeDtypeStruct((rows, plane), jnp.float32),
        in_specs=vmem(6),
        out_specs=vmem(1)[0],
        scratch_shapes=[
            pltpu.VMEM((depth, wide), jnp.float32),
            pltpu.VMEM((padded, LANES), bf16),
            pltpu.VMEM((depth, back_block), bf16),
            pltpu.VMEM((wide, back_block), bf16),
        ],
        compiler_params=params,
        cost_estimate=pl.CostEstimate(
            flops=6 * rows * plane * count, bytes_accessed=6 * rows * plane, transcendentals=0),
        name="back",
    )(w, cells, sources, kz, ky, kx)
    return out[None]


def solution(mesh):
    return jax.shard_map(
        local,
        mesh=mesh,
        in_specs=(
            P("mem", "gx", None),
            P(None, "mem", "gx", None),
            P("gx"),
            P("gx"),
            P("gx"),
            P("gx"),
            P("gx"),
        ),
        out_specs=P("mem", "gx", None),
        check_vma=False,
    )
```
